32 devices in a mesh: groups: 2 (over x), ctx: 8 (over z, y), head: 2 (over core).
Axes of the slice: x: 2, y: 2, z: 4, core: 2. Of those that a mesh axis runs over, the one named last changes fastest.
Arguments:
- prefix_x: bfloat16 [2048, 4096], P(('groups', 'ctx'), 'head'), parts along dimension 0, may hold values from -6 to 6
- prefix_z: bfloat16 [2048, 4096], P(('groups', 'ctx'), 'head'), parts along dimension 0, may hold values from -6 to 6
- prefix_b: bfloat16 [2048, 1024], P(('groups', 'ctx'), 'head'), parts along dimension 0, may hold values from -0.59765625 to 0.59765625
- prefix_c: bfloat16 [2048, 1024], P(('groups', 'ctx'), 'head'), parts along dimension 0, may hold values from -0.59765625 to 0.59765625
- prefix_decay: float32 [64, 2048], P('head', ('groups', 'ctx')), parts along dimension 1, may hold values from -0.7 to 0
- crit_x: bfloat16 [2048, 4096], P(('groups', 'ctx'), 'head'), parts along dimension 0, may hold values from -6 to 6
- crit_z: bfloat16 [2048, 4096], P(('groups', 'ctx'), 'head'), parts along dimension 0, may hold values from -6 to 6
- crit_b: bfloat16 [2048, 1024], P(('groups', 'ctx'), 'head'), parts along dimension 0, may hold values from -0.59765625 to 0.59765625
- crit_c: bfloat16 [2048, 1024], P(('groups', 'ctx'), 'head'), parts along dimension 0, may hold values from -0.59765625 to 0.59765625
- crit_decay: float32 [64, 2048], P('head', ('groups', 'ctx')), parts along dimension 1, may hold values from -0.7 to 0
- skip_weight: float32 [64], P('head'), may hold values from 0.5 to 1.5
- norm_gain: float32 [4096], P('head'), may hold values from 0.5 to 1.5
- crit_lengths: int32 [16], P(('groups', 'ctx')), parts along dimension 0, may hold values from 1 to 128, 768 in all
- crit_queries: bfloat16 [2048, 4096], P(('groups', 'ctx'), 'head'), parts along dimension 0, may hold values from -6 to 6
- crit_keys: bfloat16 [2048, 512], P(('groups', 'ctx'), 'head'), parts along dimension 0, may hold values from -6 to 6
- crit_values: bfloat16 [2048, 512], P(('groups', 'ctx'), 'head'), parts along dimension 0, may hold values from -6 to 6
- prefix_keys: bfloat16 [2048, 512], P(('groups', 'ctx'), 'head'), parts along dimension 0, may hold values from -6 to 6
- prefix_values: bfloat16 [2048, 512], P(('groups', 'ctx'), 'head'), parts along dimension 0, may hold values from -6 to 6
Outputs:
- prefix_mixed: bfloat16 [2048, 4096], P(('groups', 'ctx'), 'head'), parts along dimension 0
- crit_mixed: bfloat16 [2048, 4096], P(('groups', 'ctx'), 'head'), parts along dimension 0
- attended: bfloat16 [2048, 4096], P(('groups', 'ctx'), 'head'), parts along dimension 0
The draws below stay inside these ranges and needn't reach their ends.
There are 2 independent parts, one for each index of `groups`. The reference program is written for one: setup_inputs(seed, part) draws one part's arguments, and reference() takes and returns one part's arrays. A program takes and returns all parts, laid end to end along the dimension named above; an argument that names none is the same for every part. Nothing has to cross between parts.
Inputs may be any that keep to these rules, and one draw needn't show every extreme that they name: Critique c holds crit_lengths[c] real tokens from slot c * 128 on; the rest of its slots are padding.
All inputs are finite; a program needn't handle non-finite values. No bound on the sum of `crit_lengths` on one device may be relied on, other than what follows from the above.
Results may differ from the reference program's by a relative error of at most 0.009.
Values may be sent and summed in bfloat16 or wider, within the bound.
A program may use at most 128 MiB of HBM per device.

```python
import math
import jax
import jax.numpy as jnp
import numpy as np
from jax import lax

H = 64
P_SIZE = 64
NS = 128
G = 8
HQ = 32
KVH = 4
DH = 128
PRE_DEV = 128
CQ = 128
CRITS = 8
LP = 1024
CTOK = 1024
N_CTX = 8


def slow_heads(key):
    order = jax.random.permutation(jax.random.fold_in(key, 11), G)
    fast_count = G // 2
    slow_group = order >= fast_count
    return jnp.repeat(slow_group, H // G)


def decay_law(key, length, block, salt):
    gentle_decay = slow_heads(key)
    streams = jax.random.split(jax.random.fold_in(key, salt), 5)
    fast_rate = jnp.exp(jax.random.uniform(streams[0], (H, 1, 1), minval=math.log(1.0 / 45.0), maxval=math.log(1.0 / 40.0)))
    rate = jnp.where(gentle_decay[:, None, None], 0.3 / LP, fast_rate)
    blocks = length // block
    block_factor = jnp.exp(jax.random.uniform(streams[1], (H, blocks, 1), minval=math.log(0.5), maxval=math.log(2.0)))
    token_factor = jnp.exp(jax.random.uniform(streams[2], (H, blocks, block), minval=math.log(0.5), maxval=math.log(2.0)))
    constant_heads = -(rate * block_factor * token_factor).reshape(H, length)
    spots = jax.random.randint(streams[3], (H, 3), 0, length)
    token_positions = jnp.arange(length)[None, None, :] == spots[:, :, None]
    spike_heads = jnp.any(token_positions, axis=1) & gentle_decay[:, None]
    removed_tokens = jnp.log(jax.random.uniform(streams[4], (H, length), minval=0.5, maxval=0.8))
    return jnp.where(spike_heads, removed_tokens, constant_heads).astype(jnp.float32)


def draw_prefix_decay(key, part):
    return decay_law(key, LP, PRE_DEV, 21)


def draw_crit_decay(key, part):
    return decay_law(key, CTOK, CQ, 22)


def draw_prefix_x(key, part):
    gentle_decay = slow_heads(key)
    streams = jax.random.split(jax.random.fold_in(key, 51), 3)
    blocks = LP // PRE_DEV
    loud = jax.random.bernoulli(streams[0], 0.5, (blocks, G))
    level = jax.random.uniform(streams[1], (blocks, G))
    log_scale = jnp.where(loud, level, level - 3.0)
    group_scale = jnp.repeat(jnp.exp(log_scale), H // G, axis=1)
    head_scale = jnp.where(gentle_decay[None, :], 1.0, group_scale)
    noise = jax.random.normal(streams[2], (blocks, PRE_DEV, H, P_SIZE))
    values = jnp.clip(noise * head_scale[:, None, :, None], -6.0, 6.0)
    return values.reshape(LP, H * P_SIZE).astype(jnp.bfloat16)


def draw_crit_queries(key, part):
    noise_key = jax.random.fold_in(key, 41)
    values = jnp.clip(2.5 * jax.random.normal(noise_key, (CTOK, HQ * DH)), -6.0, 6.0)
    return values.astype(jnp.bfloat16)


def draw_prefix_keys(key, part):
    noise_key = jax.random.fold_in(key, 43)
    values = jnp.clip(jax.random.normal(noise_key, (LP, KVH * DH)), -6.0, 6.0)
    return values.astype(jnp.bfloat16)


def block_scale(key, dims, cuts, low, top_value):
    factor_of, own = 1.0, jax.random.fold_in(key, 6)
    for axis_at, shards_of in cuts:
        steps = jnp.exp(jax.random.uniform(jax.random.fold_in(own, axis_at), (shards_of,), jnp.float32, low / len(cuts), top_value / len(cuts)))
        factor_of = factor_of * jnp.repeat(steps, dims[axis_at] // shards_of).reshape([-1 if axis == axis_at else 1 for axis in range(len(dims))])
    return factor_of


def profile(count, total, reach, skew):
    weights = [(1 << 20) // math.isqrt(grade ** skew) + 1 for grade in range(2, count + 1)]
    rest, given = total - reach - (count - 1), [1] * (count - 1)
    while rest > 0:
        movable = [i for i in range(count - 1) if given[i] < reach]
        whole, budget = sum([weights[i] for i in movable]), rest
        for i in movable:
            addition = min(reach - given[i], max(1, budget * weights[i] // whole), rest)
            given[i] = given[i] + addition
            rest = rest - addition
    return np.array([reach] + given)


def uneven_parts(own_key, amount, total, limit, lean):
    if amount == 2:
        one = jax.random.randint(own_key, (), max(1, total - limit), min(limit, total - 1) + 1)
        return jnp.stack([one, total - one])
    tallies = jnp.asarray(profile(amount, total, limit, lean), jnp.int32)
    couples = (amount - 1) // 2
    donor, receiver = tallies[1:1 + 2 * couples:2], tallies[2:2 + 2 * couples:2]
    slack = jnp.minimum(donor - 1, limit - receiver)
    passed = jax.random.randint(jax.random.fold_in(own_key, 1), (couples,), 0, 1 << 20) % (slack + 1)
    tallies = tallies.at[1:1 + 2 * couples:2].set(donor - passed).at[2:2 + 2 * couples:2].set(receiver + passed)
    return tallies[jax.random.permutation(jax.random.fold_in(own_key, 2), amount)]


def scatter_about(stream_key, extent, deviation, reach, cuts=(), held_as=jnp.bfloat16):
    level = block_scale(stream_key, extent, cuts, -0.22, 0.18) if cuts else 1.0
    result = jax.random.normal(stream_key, extent, jnp.float32) * deviation * level
    return jnp.minimum(jnp.maximum(result, -reach), reach).astype(held_as)


def setup_inputs(seed: int = 0, part: int = 0) -> dict:
    key_of = jax.random.split(jax.random.key(seed), 19)
    part_splits = jax.random.split(jax.random.fold_in(key_of[18], part), 19)
    return {
        "prefix_x": draw_prefix_x(jax.random.fold_in(jax.random.fold_in(key_of[18], part), 71), part),
        "prefix_z": scatter_about(part_splits[1], (LP, H * P_SIZE), 1.0, 6.0, ((0, 8), (1, 2))),
        "prefix_b": scatter_about(part_splits[2], (LP, G * NS), 0.1, 0.59765625, ((0, 8), (1, 2))),
        "prefix_c": scatter_about(part_splits[3], (LP, G * NS), 0.1, 0.59765625, ((0, 8), (1, 2))),
        "prefix_decay": draw_prefix_decay(jax.random.fold_in(jax.random.fold_in(key_of[18], part), 71), part),
        "crit_x": scatter_about(part_splits[5], (CTOK, H * P_SIZE), 1.0, 6.0, ((0, 8), (1, 2))),
        "crit_z": scatter_about(part_splits[6], (CTOK, H * P_SIZE), 1.0, 6.0, ((0, 8), (1, 2))),
        "crit_b": scatter_about(part_splits[7], (CTOK, G * NS), 0.1, 0.59765625, ((0, 8), (1, 2))),
        "crit_c": scatter_about(part_splits[8], (CTOK, G * NS), 0.1, 0.59765625, ((0, 8), (1, 2))),
        "crit_decay": draw_crit_decay(jax.random.fold_in(jax.random.fold_in(key_of[18], part), 71), part),
        "skip_weight": jnp.clip(0.5 + 1.0 * jax.random.uniform(key_of[10], (H,), jnp.float32) ** block_scale(key_of[10], (H,), ((0, 2),), -0.2, 0.2), 0.5, 1.5),
        "norm_gain": jnp.clip(1.0 + 0.1 * jax.random.normal(key_of[11], (H * P_SIZE,), jnp.float32), 0.5, 1.5),
        "crit_lengths": uneven_parts(part_splits[12], CRITS, CRITS * CQ * 3 // 4, CQ, 1).astype(jnp.int32),
        "crit_queries": draw_crit_queries(jax.random.fold_in(jax.random.fold_in(key_of[18], part), 71), part),
        "crit_keys": scatter_about(part_splits[14], (CTOK, KVH * DH), 1.0, 6.0, ((0, 8), (1, 2))),
        "crit_values": scatter_about(part_splits[15], (CTOK, KVH * DH), 1.0, 6.0, ((0, 8), (1, 2))),
        "prefix_keys": draw_prefix_keys(jax.random.fold_in(jax.random.fold_in(key_of[18], part), 71), part),
        "prefix_values": scatter_about(part_splits[17], (LP, KVH * DH), 1.0, 6.0, ((0, 8), (1, 2))),
    }


norm_eps = 1e-05

def pieces(x_rows, b_rows, c_rows, log_decay):
    steps = x_rows.shape[0]
    per_group = H // G
    cumulative = jnp.cumsum(log_decay, axis=1)
    cum_group = cumulative.reshape(G, per_group, steps)
    inputs = x_rows.reshape(steps, G, per_group, P_SIZE).astype(jnp.float32)
    b_group = b_rows.reshape(steps, G, NS).astype(jnp.float32)
    c_group = c_rows.reshape(steps, G, NS).astype(jnp.float32)
    inner = jnp.einsum('tgn,sgn->gts', c_group, b_group)
    later = lax.broadcasted_iota(jnp.int32, (steps, steps), 0) >= lax.broadcasted_iota(jnp.int32, (steps, steps), 1)
    gap = cum_group[:, :, :, None] - cum_group[:, :, None, :]
    mixing = jnp.where(later, jnp.exp(jnp.where(later, gap, 0.0)), 0.0) * inner[:, None]
    mixing = lax.optimization_barrier(mixing.astype(jnp.bfloat16)).astype(jnp.float32)
    within = jnp.einsum('gkts,sgkp->tgkp', mixing, inputs)
    tail = jnp.transpose(jnp.exp(cum_group[:, :, -1:] - cum_group), (2, 0, 1))[..., None]
    scaled = lax.optimization_barrier((inputs * tail).astype(jnp.bfloat16)).astype(jnp.float32)
    local_state = jnp.einsum('sgkp,sgn->gkpn', scaled, b_group).reshape(H, P_SIZE, NS)
    return (cumulative, within, local_state)

def finish(within, cumulative, entry, x_rows, c_rows, z_rows, skip_weight, norm_gain):
    steps = x_rows.shape[0]
    per_group = H // G
    c_group = c_rows.reshape(steps, G, NS).astype(jnp.float32)
    across = jnp.einsum('tgn,gkpn->tgkp', c_group, entry.reshape(G, per_group, P_SIZE, NS), precision=lax.Precision.HIGHEST)
    growth = jnp.transpose(jnp.exp(cumulative.reshape(G, per_group, steps)), (2, 0, 1))[..., None]
    inputs = x_rows.reshape(steps, G, per_group, P_SIZE).astype(jnp.float32)
    output_rows = within + across * growth + skip_weight.reshape(G, per_group, 1) * inputs
    gated = output_rows * jax.nn.silu(z_rows.reshape(steps, G, per_group, P_SIZE).astype(jnp.float32))
    power = lax.optimization_barrier(jnp.mean(gated * gated, axis=(2, 3), keepdims=True))
    normed = gated * lax.rsqrt(power + norm_eps) * norm_gain.reshape(G, per_group, P_SIZE)
    return normed.reshape(steps, H * P_SIZE)

def reference(prefix_x, prefix_z, prefix_b, prefix_c, prefix_decay, crit_x, crit_z, crit_b, crit_c, crit_decay, skip_weight, norm_gain, crit_lengths, crit_queries, crit_keys, crit_values, prefix_keys, prefix_values):
    width = H * P_SIZE
    columns = G * NS
    prefix_parts = (prefix_x.reshape(N_CTX, PRE_DEV, width), prefix_z.reshape(N_CTX, PRE_DEV, width), prefix_b.reshape(N_CTX, PRE_DEV, columns), prefix_c.reshape(N_CTX, PRE_DEV, columns), jnp.transpose(prefix_decay.reshape(H, N_CTX, PRE_DEV), (1, 0, 2)))

    def advance(entry, block):
        x_rows, z_rows, b_rows, c_rows, log_decay = block
        cumulative, within, local_state = pieces(x_rows, b_rows, c_rows, log_decay)
        mixed = finish(within, cumulative, entry, x_rows, c_rows, z_rows, skip_weight, norm_gain).astype(jnp.bfloat16)
        carried = jnp.exp(cumulative[:, -1])[:, None, None] * entry + local_state
        return (carried, mixed)
    final_state, prefix_blocks = lax.scan(advance, jnp.zeros((H, P_SIZE, NS), jnp.float32), prefix_parts)
    prefix_mixed = prefix_blocks.reshape(LP, width)
    positions = lax.broadcasted_iota(jnp.int32, (CQ, 1), 0)

    def critique(block):
        x_rows, z_rows, b_rows, c_rows, log_decay, length = block
        cumulative, within, unused = pieces(x_rows, b_rows, c_rows, log_decay)
        mixed = finish(within, cumulative, final_state, x_rows, c_rows, z_rows, skip_weight, norm_gain)
        return jnp.where(positions < length, mixed, 0.0).astype(jnp.bfloat16)
    crit_parts = (crit_x.reshape(CRITS, CQ, width), crit_z.reshape(CRITS, CQ, width), crit_b.reshape(CRITS, CQ, columns), crit_c.reshape(CRITS, CQ, columns), jnp.transpose(crit_decay.reshape(H, CRITS, CQ), (1, 0, 2)), crit_lengths)
    crit_mixed = lax.map(critique, crit_parts).reshape(CTOK, width)
    ratio = HQ // KVH
    scale = DH ** (-0.5)
    cached_keys = prefix_keys.reshape(LP, KVH, DH).astype(jnp.float32)
    cached_values = prefix_values.reshape(LP, KVH, DH).astype(jnp.float32)
    key_index = lax.broadcasted_iota(jnp.int32, (CQ, LP + CQ), 1)
    query_index = lax.broadcasted_iota(jnp.int32, (CQ, LP + CQ), 0)
    visible = (key_index < LP) | (key_index - LP <= query_index)

    def attend(block):
        queries, keys, values, length = block
        queries = queries.reshape(CQ, KVH, ratio, DH).astype(jnp.float32)
        all_keys = jnp.concatenate([cached_keys, keys.reshape(CQ, KVH, DH).astype(jnp.float32)], axis=0)
        all_values = jnp.concatenate([cached_values, values.reshape(CQ, KVH, DH).astype(jnp.float32)], axis=0)
        scores = jnp.einsum('qgrd,kgd->qgrk', queries, all_keys) * scale
        scores = jnp.where(visible[:, None, None, :], scores, -jnp.inf)
        probs = jnp.exp(scores - lax.optimization_barrier(jnp.max(scores, axis=-1, keepdims=True)))
        mass = lax.optimization_barrier(jnp.sum(probs, axis=-1))
        probs_low = lax.optimization_barrier(probs.astype(jnp.bfloat16)).astype(jnp.float32)
        summed = jnp.einsum('qgrk,kgd->qgrd', probs_low, all_values)
        output_rows = (summed / mass[..., None]).reshape(CQ, HQ * DH)
        return jnp.where(positions < length, output_rows, 0.0).astype(jnp.bfloat16)
    attend_parts = (crit_queries.reshape(CRITS, CQ, HQ * DH), crit_keys.reshape(CRITS, CQ, KVH * DH), crit_values.reshape(CRITS, CQ, KVH * DH), crit_lengths)
    attended = lax.map(attend, attend_parts).reshape(CTOK, HQ * DH)
    return (prefix_mixed, crit_mixed, attended)
```

```python
import functools
import math

import jax
import jax.numpy as jnp
from jax import lax
from jax.experimental import pallas as pl
from jax.experimental.pallas import tpu as pltpu
from jax.sharding import PartitionSpec as P

NS = 128
DH = 128
NORM_EPS = 1e-05
CHUNKS = 4
LOG2E = 1.4426950408889634
MESH = pl.DeviceIdType.MESH
HI = lax.Precision.HIGHEST
F32 = jnp.float32
BF16 = jnp.bfloat16


def nt(a, b, precision=None):
    return lax.dot_general(
        a, b, (((1,), (1,)), ((), ())), preferred_element_type=F32, precision=precision
    )


def nn(a, b, precision=None):
    return jnp.dot(a, b, preferred_element_type=F32, precision=precision)


def kernel(
    n,
    px,
    pz,
    pb,
    pc,
    pd,
    cx,
    cz,
    cb,
    cc,
    cd,
    skip,
    gain,
    length_ref,
    q_ref,
    ck,
    cv,
    pk,
    pv,
    out_p,
    out_c,
    out_a,
    kv,
    s_own,
    s_send,
    s_in,
    pair,
    e_out,
    e_in,
    r_out,
    r_in,
    x_out,
    state,
    e_keep,
    within_p,
    within_c,
    grow_p,
    grow_c,
    cols_p,
    cols_c,
    rows_p,
    rows_c,
    skips,
    kvy_s,
    kvy_r,
    up_s,
    up_r,
    dn_s,
    dn_r,
    s_s,
    s_r,
    e_s,
    e_r,
    r_s,
    r_r,
    x_s,
    x_r,
):
    me = lax.axis_index("ctx")
    y = lax.rem(me, 2)
    z = lax.div(me, 2)
    nz = n // 2
    other = me + 1 - 2 * y
    has_up = z < nz - 1
    has_dn = z > 0
    steps = px.shape[0]
    groups = pb.shape[1] // NS
    per = pd.shape[0] // groups
    gw = px.shape[1] // groups
    width = gw // per
    cw = s_own.shape[2]
    tail_rows = s_send.shape[1] - NS

    barrier = pltpu.get_barrier_semaphore()
    pl.semaphore_signal(barrier, inc=1, device_id={"ctx": other}, device_id_type=MESH)

    @pl.when(has_up)
    def _():
        pl.semaphore_signal(barrier, inc=1, device_id={"ctx": me + 2}, device_id_type=MESH)

    @pl.when(has_dn)
    def _():
        pl.semaphore_signal(barrier, inc=1, device_id={"ctx": me - 2}, device_id_type=MESH)

    def remote(src, dst, ss, rs, to):
        return pltpu.make_async_remote_copy(
            src_ref=src,
            dst_ref=dst,
            send_sem=ss,
            recv_sem=rs,
            device_id={"ctx": to},
            device_id_type=MESH,
        )

    kv_y = remote(kv.at[me], kv.at[me], kvy_s, kvy_r, other)
    s_c = [
        remote(
            s_send.at[(1 - y) * CHUNKS + c], s_in.at[c], s_s.at[c], s_r.at[c], other
        )
        for c in range(CHUNKS)
    ]
    e_c = [remote(e_out.at[c], e_in.at[c], e_s.at[c], e_r.at[c], me + 2) for c in range(CHUNKS)]
    r_c = [remote(r_out.at[c], r_in.at[c], r_s.at[c], r_r.at[c], me - 2) for c in range(CHUNKS)]
    x_c = [
        remote(x_out.at[c], state.at[y * CHUNKS + c], x_s.at[c], x_r.at[c], other)
        for c in range(CHUNKS)
    ]

    def kv_up(j):
        at = kv.at[pl.ds(2 * (z - j), 2)]
        return remote(at, at, up_s.at[j], up_r.at[j], me + 2)

    def kv_dn(j):
        at = kv.at[pl.ds(2 * (z + j), 2)]
        return remote(at, at, dn_s.at[j], dn_r.at[j], me - 2)

    def kv_send(j):
        @pl.when(jnp.logical_and(has_up, z - j >= 0))
        def _():
            kv_up(j).start()

        @pl.when(jnp.logical_and(has_dn, z + j < nz))
        def _():
            kv_dn(j).start()

    def kv_recv(j):
        @pl.when(z - 1 - j >= 0)
        def _():
            at = kv.at[pl.ds(2 * (z - 1 - j), 2)]
            remote(at, at, up_s.at[j], up_r.at[j], me + 2).wait_recv()

        @pl.when(z + 1 + j < nz)
        def _():
            at = kv.at[pl.ds(2 * (z + 1 + j), 2)]
            remote(at, at, dn_s.at[j], dn_r.at[j], me - 2).wait_recv()

    kv[me, 0] = pk[...]
    kv[me, 1] = pv[...]
    t_at = lax.broadcasted_iota(jnp.int32, (steps, steps), 0)
    s_at = lax.broadcasted_iota(jnp.int32, (steps, steps), 1)
    later = t_at >= s_at
    tri = jnp.where(later, 1.0, 0.0)
    spread = jnp.where(
        lax.broadcasted_iota(jnp.int32, (per, gw), 1) // width
        == lax.broadcasted_iota(jnp.int32, (per, gw), 0),
        1.0,
        0.0,
    )
    rows_p[...] = nt(pd[...], tri, HI)
    rows_c[...] = nt(cd[...], tri, HI)
    half_chunks = gw // cw
    for g in range(groups):
        col = nt(tri, pd[g * per : (g + 1) * per, :], HI)
        cols_p[g] = col
        cols_c[g] = nt(tri, cd[g * per : (g + 1) * per, :], HI)
        grow = nn(jnp.exp(col), spread, HI)
        grow_p[g] = grow
        tail = nn(jnp.exp(col[steps - 1 : steps, :] - col), spread, HI)
        lanes = slice(g * gw, (g + 1) * gw)
        scaled = (px[:, lanes].astype(F32) * tail).astype(BF16)
        b_t = pb[:, g * NS : (g + 1) * NS].astype(F32).T.astype(BF16)
        local = nn(b_t, scaled)
        low = local.astype(BF16)
        last = jnp.broadcast_to(grow[steps - 1 : steps, :], (8, gw))
        last_hi = last.astype(BF16)
        last_lo = (last - last_hi.astype(F32)).astype(BF16)
        code = jnp.concatenate([last_hi, last_lo], axis=0)
        for k in range(half_chunks):
            at = g * half_chunks + k
            s_own[at] = local[:, k * cw : (k + 1) * cw]
            s_send[at, 0:NS] = low[:, k * cw : (k + 1) * cw]
            s_send[at, NS : NS + tail_rows] = code[:, k * cw : (k + 1) * cw]
        skips[g] = nn(jnp.broadcast_to(skip[:, g * per : (g + 1) * per], (8, per)), spread, HI)

    peers = 1 + jnp.where(has_up, 1, 0) + jnp.where(has_dn, 1, 0)
    pl.semaphore_wait(barrier, peers)

    s_c[0].start()
    kv_y.start()
    for c in range(1, CHUNKS):
        s_c[c].start()

    lane = lax.broadcasted_iota(jnp.int32, (steps, 2 * width), 1)

    def within(x_ref, b_ref, c_ref, cols, rows, result):
        def group(g, carry):
            off = pl.multiple_of(g * NS, NS)
            inner = nt(c_ref[:, pl.ds(off, NS)], b_ref[:, pl.ds(off, NS)])
            col = cols[g]
            row = rows[pl.ds(pl.multiple_of(g * per, per), per), :]
            for k in range(per // 2):
                mixed = []
                for h in (2 * k, 2 * k + 1):
                    gap = col[:, h : h + 1] - row[h : h + 1, :]
                    mixed.append(
                        (jnp.exp(jnp.where(later, gap, -jnp.inf)) * inner).astype(BF16)
                    )
                xs = x_ref[:, pl.ds(pl.multiple_of(g * gw + k * 2 * width, NS), 2 * width)]
                zero = jnp.zeros_like(xs)
                both = jnp.concatenate(
                    [jnp.where(lane < width, xs, zero), jnp.where(lane < width, zero, xs)], axis=0
                )
                result[g, :, k * 2 * width : (k + 1) * 2 * width] = nn(
                    jnp.concatenate(mixed, axis=1), both
                )
            return carry

        lax.fori_loop(0, groups, group, 0)

    within(px, pb, pc, cols_p, rows_p, within_p)

    kv_y.wait_recv()
    kv_send(0)

    def decode(ref, c):
        return ref[c, NS : NS + 1].astype(F32) + ref[c, NS + 8 : NS + 9].astype(F32)

    def own_decay(c):
        at = y * CHUNKS + c
        return s_send[at, NS : NS + 1].astype(F32) + s_send[at, NS + 8 : NS + 9].astype(F32)

    def pair_decay(c):
        return own_decay(c) * decode(s_in, c)

    for c in range(CHUNKS):
        s_c[c].wait_recv()
        mine = s_own[y * CHUNKS + c]
        his = s_in[c, 0:NS].astype(F32)
        pair[c] = jnp.where(y == 0, his + decode(s_in, c) * mine, mine + own_decay(c) * his)

        @pl.when(jnp.logical_not(has_dn))
        def _():
            e_out[c] = pair[c].astype(BF16)
            e_keep[c] = jnp.zeros_like(e_keep[c])
            e_c[c].start()

        @pl.when(jnp.logical_not(has_up))
        def _():
            r_out[c, 0:NS] = pair[c].astype(BF16)
            code_decay(r_out, c, pair_decay(c))
            r_c[c].start()

    def chain_e(c):
        @pl.when(has_dn)
        def _():
            e_c[c].wait_recv()
            got = e_in[c].astype(F32)
            e_keep[c] = got

            @pl.when(has_up)
            def _():
                e_out[c] = (pair_decay(c) * got + pair[c]).astype(BF16)
                e_c[c].start()

    def chain_r(c):
        @pl.when(has_up)
        def _():
            r_c[c].wait_recv()

            @pl.when(has_dn)
            def _():
                after = decode(r_in, c)
                r_out[c, 0:NS] = (after * pair[c] + r_in[c, 0:NS].astype(F32)).astype(BF16)
                code_decay(r_out, c, after * pair_decay(c))
                r_c[c].start()

    def settle(c):
        at = y * CHUNKS + c
        entry = e_keep[c]
        through = pair_decay(c) * entry + pair[c]

        @pl.when(has_up)
        def _():
            x_out[c, 1] = (
                decode(r_in, c) * through + r_in[c, 0:NS].astype(F32)
            ).astype(BF16)

        @pl.when(jnp.logical_not(has_up))
        def _():
            x_out[c, 1] = through.astype(BF16)

        state[at, 1] = x_out[c, 1]
        first = entry.astype(BF16)

        @pl.when(y == 0)
        def _():
            state[at, 0] = first
            x_out[c, 0] = (own_decay(c) * entry + s_own[at]).astype(BF16)

        @pl.when(y != 0)
        def _():
            x_out[c, 0] = first
            state[at, 0] = (decode(s_in, c) * entry + s_in[c, 0:NS].astype(F32)).astype(BF16)

        x_c[c].start()

    low_half = 2 * z < nz

    @pl.when(low_half)
    def _():
        for c in range(CHUNKS):
            chain_e(c)

    @pl.when(jnp.logical_not(low_half))
    def _():
        for c in range(CHUNKS):
            chain_r(c)

    if nz > 1:
        kv_recv(0)
        if nz > 2:
            kv_send(1)

    @pl.when(low_half)
    def _():
        for c in range(CHUNKS):
            chain_r(c)

    @pl.when(jnp.logical_not(low_half))
    def _():
        for c in range(CHUNKS):
            chain_e(c)

    for c in range(CHUNKS):
        settle(c)

    for g in range(groups):
        grow_c[g] = nn(jnp.exp(cols_c[g]), spread, HI)
    within(cx, cb, cc, cols_c, rows_c, within_c)

    for j in range(1, nz - 1):
        kv_recv(j)
        if j + 1 < nz - 1:
            kv_send(j + 1)

    length = length_ref[0]
    real = lax.broadcasted_iota(jnp.int32, (steps, 1), 0) < length
    kv_heads = ck.shape[1] // DH
    ratio = q_ref.shape[1] // (DH * kv_heads)
    factor = DH ** (-0.5) * LOG2E
    span = math.gcd(n, 8)

    for g in range(kv_heads):
        cols = slice(g * DH, (g + 1) * DH)

        def head(j, carry):
            at = pl.ds(pl.multiple_of((g * ratio + j) * DH, DH), DH)
            q = q_ref[:, at]
            s = jnp.where(later, nt(q, ck[:, cols]), -jnp.inf)
            best = jnp.max(s, axis=1, keepdims=True)
            p = jnp.exp2((s - best) * factor)
            mass = jnp.sum(p, axis=1, keepdims=True)
            acc = nn(p.astype(BF16), cv[:, cols])

            def visit(b, part):
                best, mass, acc = part
                keys = kv[pl.ds(b * span, span), 0, :, cols].reshape(span * steps, DH)
                vals = kv[pl.ds(b * span, span), 1, :, cols].reshape(span * steps, DH)
                s = nt(q, keys)
                new = jnp.maximum(best, jnp.max(s, axis=1, keepdims=True))
                p = jnp.exp2((s - new) * factor)
                fade = jnp.exp2((best - new) * factor)
                mass = mass * fade + jnp.sum(p, axis=1, keepdims=True)
                return new, mass, acc * fade + nn(p.astype(BF16), vals)

            part = (best, mass, acc)
            if n == span:
                part = visit(0, part)
            else:
                part = lax.fori_loop(0, n // span, visit, part)
            best, mass, acc = part
            out_a[:, at] = jnp.where(real, acc / mass, 0.0).astype(BF16)
            return carry

        lax.fori_loop(0, ratio, head, 0)

    for c in range(CHUNKS):
        remote(
            x_out.at[c], state.at[(1 - y) * CHUNKS + c], x_s.at[c], x_r.at[c], other
        ).wait_recv()

    def finish(g, carry):
        lanes = pl.ds(pl.multiple_of(g * gw, gw), gw)
        off = pl.ds(pl.multiple_of(g * NS, NS), NS)
        for which, (x_ref, z_ref, c_ref, wi, gr, out) in enumerate(
            ((px, pz, pc, within_p, grow_p, out_p), (cx, cz, cc, within_c, grow_c, out_c))
        ):
            c_rows = c_ref[:, off]
            across = jnp.concatenate(
                [nn(c_rows, state[g * half_chunks + k, which]) for k in range(half_chunks)], axis=1
            )
            rows = wi[g] + across * gr[g] + skips[g, 0:1] * x_ref[:, lanes].astype(F32)
            gate = z_ref[:, lanes].astype(F32)
            gated = rows * (gate / (1.0 + jnp.exp(-gate)))
            power = jnp.sum(gated * gated, axis=1, keepdims=True) * (1.0 / gw)
            normed = gated * lax.rsqrt(power + NORM_EPS) * gain[:, lanes]
            if which == 1:
                normed = jnp.where(real, normed, 0.0)
            out[:, lanes] = normed.astype(BF16)
        return carry

    lax.fori_loop(0, groups, finish, 0)

    kv_y.wait_send()
    for c in range(CHUNKS):
        s_c[c].wait_send()
        x_c[c].wait_send()

    @pl.when(has_up)
    def _():
        for c in range(CHUNKS):
            e_c[c].wait_send()

    @pl.when(has_dn)
    def _():
        for c in range(CHUNKS):
            r_c[c].wait_send()

    for j in range(nz - 1):

        @pl.when(jnp.logical_and(has_up, z - j >= 0))
        def _():
            kv_up(j).wait_send()

        @pl.when(jnp.logical_and(has_dn, z + j < nz))
        def _():
            kv_dn(j).wait_send()


def code_decay(ref, c, value):
    value = jnp.broadcast_to(value, (8, value.shape[1]))
    high = value.astype(BF16)
    ref[c, NS : NS + 16] = jnp.concatenate([high, (value - high.astype(F32)).astype(BF16)], axis=0)


def shards(n, *args):
    args = list(args)
    args[10] = args[10].reshape(1, -1)
    args[11] = args[11].reshape(1, -1)
    px, pb, pd, pk = args[0], args[2], args[4], args[16]
    steps, hp = px.shape
    groups = pb.shape[1] // NS
    heads = pd.shape[0]
    gw = hp // groups
    per = heads // groups
    cw = hp // (2 * CHUNKS)
    nz = n // 2
    full = pl.BlockSpec(memory_space=pltpu.VMEM)
    in_specs = [full] * len(args)
    in_specs[12] = pl.BlockSpec(memory_space=pltpu.SMEM)
    dma = pltpu.SemaphoreType.DMA
    links = max(nz - 1, 1)
    scratch = [
        pltpu.VMEM((n, 2) + pk.shape, BF16),
        pltpu.VMEM((2 * CHUNKS, NS, cw), F32),
        pltpu.VMEM((2 * CHUNKS, NS + 16, cw), BF16),
        pltpu.VMEM((CHUNKS, NS + 16, cw), BF16),
        pltpu.VMEM((CHUNKS, NS, cw), F32),
        pltpu.VMEM((CHUNKS, NS, cw), BF16),
        pltpu.VMEM((CHUNKS, NS, cw), BF16),
        pltpu.VMEM((CHUNKS, NS + 16, cw), BF16),
        pltpu.VMEM((CHUNKS, NS + 16, cw), BF16),
        pltpu.VMEM((CHUNKS, 2, NS, cw), BF16),
        pltpu.VMEM((2 * CHUNKS, 2, NS, cw), BF16),
        pltpu.VMEM((CHUNKS, NS, cw), F32),
        pltpu.VMEM((groups, steps, gw), F32),
        pltpu.VMEM((groups, steps, gw), F32),
        pltpu.VMEM((groups, steps, gw), F32),
        pltpu.VMEM((groups, steps, gw), F32),
        pltpu.VMEM((groups, steps, per), F32),
        pltpu.VMEM((groups, steps, per), F32),
        pltpu.VMEM((heads, steps), F32),
        pltpu.VMEM((heads, steps), F32),
        pltpu.VMEM((groups, 8, gw), F32),
        dma,
        dma,
        dma((links,)),
        dma((links,)),
        dma((links,)),
        dma((links,)),
    ] + [dma((CHUNKS,))] * 8
    out = jax.ShapeDtypeStruct(px.shape, BF16)
    return pl.pallas_call(
        functools.partial(kernel, n),
        out_shape=(out, out, out),
        in_specs=in_specs,
        out_specs=(full, full, full),
        scratch_shapes=scratch,
        compiler_params=pltpu.CompilerParams(
            collective_id=0, has_side_effects=True, vmem_limit_bytes=56 * 2**20
        ),
    )(*args)


def solution(mesh):
    rows = P(("groups", "ctx"), "head")
    cols = P("head", ("groups", "ctx"))
    in_specs = (
        (rows,) * 4
        + (cols,)
        + (rows,) * 4
        + (cols, P("head"), P("head"), P(("groups", "ctx")))
        + (rows,) * 5
    )
    return jax.shard_map(
        functools.partial(shards, mesh.shape["ctx"]),
        mesh=mesh,
        in_specs=in_specs,
        out_specs=(rows, rows, rows),
        check_vma=False,
    )
```

```python
import functools
import math

import jax
import jax.numpy as jnp
from jax import lax
from jax.experimental import pallas as pl
from jax.experimental.pallas import tpu as pltpu
from jax.sharding import PartitionSpec as P

NS = 128
DH = 128
NORM_EPS = 1e-05
CHUNKS = 8
LAG = 2
LOG2E = 1.4426950408889634
MESH = pl.DeviceIdType.MESH
HI = lax.Precision.HIGHEST
F32 = jnp.float32
BF16 = jnp.bfloat16


def nt(a, b, precision=None):
    return lax.dot_general(
        a, b, (((1,), (1,)), ((), ())), preferred_element_type=F32, precision=precision
    )


def nn(a, b, precision=None):
    return jnp.dot(a, b, preferred_element_type=F32, precision=precision)


def kernel(
    n,
    px,
    pz,
    pb,
    pc,
    pd,
    cx,
    cz,
    cb,
    cc,
    cd,
    skip,
    gain,
    length_ref,
    q_ref,
    ck,
    cv,
    pk,
    pv,
    out_p,
    out_c,
    out_a,
    kv,
    s_own,
    s_send,
    s_in,
    pair,
    e_out,
    e_in,
    r_out,
    r_in,
    state,
    att_acc,
    att_best,
    att_mass,
    within_p,
    within_c,
    grow_p,
    grow_c,
    cols_p,
    cols_c,
    rows_p,
    rows_c,
    skips,
    kvy_s,
    kvy_r,
    up_s,
    up_r,
    dn_s,
    dn_r,
    s_s,
    s_r,
    e_s,
    e_r,
    r_s,
    r_r,
):
    me = lax.axis_index("ctx")
    y = lax.rem(me, 2)
    z = lax.div(me, 2)
    nz = n // 2
    other = me + 1 - 2 * y
    has_up = z < nz - 1
    has_dn = z > 0
    steps = px.shape[0]
    groups = pb.shape[1] // NS
    per = pd.shape[0] // groups
    gw = px.shape[1] // groups
    width = gw // per
    cw = s_own.shape[2]
    tail_rows = s_send.shape[1] - NS

    barrier = pltpu.get_barrier_semaphore()
    pl.semaphore_signal(barrier, inc=1, device_id={"ctx": other}, device_id_type=MESH)

    @pl.when(has_up)
    def _():
        pl.semaphore_signal(barrier, inc=1, device_id={"ctx": me + 2}, device_id_type=MESH)

    @pl.when(has_dn)
    def _():
        pl.semaphore_signal(barrier, inc=1, device_id={"ctx": me - 2}, device_id_type=MESH)

    def remote(src, dst, ss, rs, to):
        return pltpu.make_async_remote_copy(
            src_ref=src,
            dst_ref=dst,
            send_sem=ss,
            recv_sem=rs,
            device_id={"ctx": to},
            device_id_type=MESH,
        )

    s_c = [remote(s_send.at[c], s_in.at[c], s_s.at[c], s_r.at[c], other) for c in range(CHUNKS)]
    e_c = [remote(e_out.at[c], e_in.at[c], e_s.at[c], e_r.at[c], me + 2) for c in range(CHUNKS)]
    r_c = [remote(r_out.at[c], r_in.at[c], r_s.at[c], r_r.at[c], me - 2) for c in range(CHUNKS)]
    links = max(nz - 1, 1)

    def kv_up(at, j):
        return remote(kv.at[y, at], kv.at[y, at], up_s.at[j], up_r.at[j], me + 2)

    def kv_dn(at, j):
        return remote(kv.at[y, at], kv.at[y, at], dn_s.at[j], dn_r.at[j], me - 2)

    def kv_side(column, at, k):
        ref = kv.at[column, at]
        return remote(ref, ref, kvy_s.at[k], kvy_r.at[k], other)

    def kv_each(j, up, down):
        pl.when(jnp.logical_and(has_up, z - j >= 0))(lambda: up(kv_up(z - j, j)))
        pl.when(jnp.logical_and(has_dn, z + j < nz))(lambda: down(kv_dn(z + j, j)))

    def kv_send(j):
        kv_each(j, lambda d: d.start(), lambda d: d.start())

    def kv_step(j):
        @pl.when(z - 1 - j >= 0)
        def _():
            kv_up(z - 1 - j, j).wait_recv()

        @pl.when(z + 1 + j < nz)
        def _():
            kv_dn(z + 1 + j, j).wait_recv()

        if j + 1 < nz - 1:
            kv_send(j + 1)
        kv_across(j, lambda at, k: kv_side(y, at, k).start())

    def kv_across(j, act):
        pl.when(z - 1 - j >= 0)(lambda: act(z - 1 - j, j))
        pl.when(z + 1 + j < nz)(lambda: act(z + 1 + j, links + j))

    kv[y, z, 0] = pk[...]
    kv[y, z, 1] = pv[...]

    @pl.when(jnp.logical_not(has_dn))
    def _():
        e_in[...] = jnp.zeros_like(e_in)

    @pl.when(jnp.logical_not(has_up))
    def _():
        for c in range(CHUNKS):
            r_in[c, 0:NS] = jnp.zeros((NS, cw), BF16)
            code_decay(r_in, c, jnp.ones((1, cw), F32))

    t_at = lax.broadcasted_iota(jnp.int32, (steps, steps), 0)
    s_at = lax.broadcasted_iota(jnp.int32, (steps, steps), 1)
    later = t_at >= s_at
    tri = jnp.where(later, 1.0, 0.0)
    spread = jnp.where(
        lax.broadcasted_iota(jnp.int32, (per, gw), 1) // width
        == lax.broadcasted_iota(jnp.int32, (per, gw), 0),
        1.0,
        0.0,
    )
    rows_p[...] = nt(pd[...], tri, HI)
    rows_c[...] = nt(cd[...], tri, HI)
    half_chunks = gw // cw
    for g in range(groups):
        col = nt(tri, pd[g * per : (g + 1) * per, :], HI)
        cols_p[g] = col
        cols_c[g] = nt(tri, cd[g * per : (g + 1) * per, :], HI)
        grow = nn(jnp.exp(col), spread, HI)
        grow_p[g] = grow
        tail = nn(jnp.exp(col[steps - 1 : steps, :] - col), spread, HI)
        lanes = slice(g * gw, (g + 1) * gw)
        scaled = (px[:, lanes].astype(F32) * tail).astype(BF16)
        b_t = pb[:, g * NS : (g + 1) * NS].astype(F32).T.astype(BF16)
        local = nn(b_t, scaled)
        low = local.astype(BF16)
        last = jnp.broadcast_to(grow[steps - 1 : steps, :], (8, gw))
        last_hi = last.astype(BF16)
        last_lo = (last - last_hi.astype(F32)).astype(BF16)
        code = jnp.concatenate([last_hi, last_lo], axis=0)
        for k in range(half_chunks):
            at = g * half_chunks + k
            s_own[at] = local[:, k * cw : (k + 1) * cw]
            s_send[at, 0:NS] = low[:, k * cw : (k + 1) * cw]
            s_send[at, NS : NS + tail_rows] = code[:, k * cw : (k + 1) * cw]
        skips[g] = nn(jnp.broadcast_to(skip[:, g * per : (g + 1) * per], (8, per)), spread, HI)

    peers = 1 + jnp.where(has_up, 1, 0) + jnp.where(has_dn, 1, 0)
    pl.semaphore_wait(barrier, peers)

    if nz > 1:
        kv_send(0)
    for c in range(CHUNKS):
        s_c[c].start()
    kv_side(y, z, 2 * links).start()

    lane = lax.broadcasted_iota(jnp.int32, (steps, 2 * width), 1)

    def within(x_ref, b_ref, c_ref, cols, rows, result):
        def group(g, carry):
            off = pl.multiple_of(g * NS, NS)
            inner = nt(c_ref[:, pl.ds(off, NS)], b_ref[:, pl.ds(off, NS)])
            col = cols[g]
            row = rows[pl.ds(pl.multiple_of(g * per, per), per), :]
            for k in range(per // 2):
                mixed = []
                for h in (2 * k, 2 * k + 1):
                    gap = col[:, h : h + 1] - row[h : h + 1, :]
                    mixed.append(
                        (jnp.exp(jnp.where(later, gap, -jnp.inf)) * inner).astype(BF16)
                    )
                xs = x_ref[:, pl.ds(pl.multiple_of(g * gw + k * 2 * width, NS), 2 * width)]
                zero = jnp.zeros_like(xs)
                both = jnp.concatenate(
                    [jnp.where(lane < width, xs, zero), jnp.where(lane < width, zero, xs)], axis=0
                )
                result[g, :, k * 2 * width : (k + 1) * 2 * width] = nn(
                    jnp.concatenate(mixed, axis=1), both
                )
            return carry

        lax.fori_loop(0, groups, group, 0)

    within(px, pb, pc, cols_p, rows_p, within_p)

    for g in range(groups):
        grow_c[g] = nn(jnp.exp(cols_c[g]), spread, HI)

    def decode(ref, c):
        return ref[c, NS : NS + 1].astype(F32) + ref[c, NS + 8 : NS + 9].astype(F32)

    def pair_decay(c):
        return decode(s_send, c) * decode(s_in, c)

    def pair_sum(c):
        s_c[c].wait_recv()
        mine = s_own[c]
        his = s_in[c, 0:NS].astype(F32)
        pair[c] = jnp.where(y == 0, his + decode(s_in, c) * mine, mine + decode(s_send, c) * his)

    def chain_e(c):
        pl.when(has_dn)(lambda: e_c[c].wait_recv())

        @pl.when(has_up)
        def _():
            e_out[c] = (pair_decay(c) * e_in[c].astype(F32) + pair[c]).astype(BF16)
            e_c[c].start()

    def chain_r(c):
        pl.when(has_up)(lambda: r_c[c].wait_recv())

        @pl.when(has_dn)
        def _():
            after = decode(r_in, c)
            r_out[c, 0:NS] = (after * pair[c] + r_in[c, 0:NS].astype(F32)).astype(BF16)
            code_decay(r_out, c, after * pair_decay(c))
            r_c[c].start()

    def settle(c):
        entry = e_in[c].astype(F32)
        through = pair_decay(c) * entry + pair[c]
        state[c, 1] = (decode(r_in, c) * through + r_in[c, 0:NS].astype(F32)).astype(BF16)

        @pl.when(y == 0)
        def _():
            state[c, 0] = e_in[c]

        @pl.when(y != 0)
        def _():
            state[c, 0] = (decode(s_in, c) * entry + s_in[c, 0:NS].astype(F32)).astype(BF16)

    length = length_ref[0]
    real = lax.broadcasted_iota(jnp.int32, (steps, 1), 0) < length
    kv_heads = ck.shape[1] // DH
    q_heads = q_ref.shape[1] // DH
    ratio = q_heads // kv_heads
    factor = DH ** (-0.5) * LOG2E
    span = math.gcd(nz, 8)

    def seen(q, cols, column, part):
        def visit(b, part):
            best, mass, acc = part
            keys = kv[column, pl.ds(b * span, span), 0, :, cols].reshape(span * steps, DH)
            vals = kv[column, pl.ds(b * span, span), 1, :, cols].reshape(span * steps, DH)
            s = nt(q, keys)
            new = jnp.maximum(best, jnp.max(s, axis=1, keepdims=True))
            p = jnp.exp2((s - new) * factor)
            fade = jnp.exp2((best - new) * factor)
            mass = mass * fade + jnp.sum(p, axis=1, keepdims=True)
            return new, mass, acc * fade + nn(p.astype(BF16), vals)

        if nz == span:
            return visit(0, part)
        return lax.fori_loop(0, nz // span, visit, part)

    def attend_own(start, stop):
        def head(j, carry):
            cols = pl.ds(pl.multiple_of(lax.div(j, ratio) * DH, DH), DH)
            q = q_ref[:, pl.ds(pl.multiple_of(j * DH, DH), DH)]
            s = jnp.where(later, nt(q, ck[:, cols]), -jnp.inf)
            best = jnp.max(s, axis=1, keepdims=True)
            p = jnp.exp2((s - best) * factor)
            mass = jnp.sum(p, axis=1, keepdims=True)
            acc = nn(p.astype(BF16), cv[:, cols])
            att_best[j], att_mass[j], att_acc[j] = seen(q, cols, y, (best, mass, acc))
            return carry

        lax.fori_loop(start, stop, head, 0)

    def attend_rest():
        def head(j, carry):
            cols = pl.ds(pl.multiple_of(lax.div(j, ratio) * DH, DH), DH)
            at = pl.ds(pl.multiple_of(j * DH, DH), DH)
            best, mass, acc = seen(
                q_ref[:, at], cols, 1 - y, (att_best[j], att_mass[j], att_acc[j])
            )
            out_a[:, at] = jnp.where(real, acc / mass, 0.0).astype(BF16)
            return carry

        lax.fori_loop(0, q_heads, head, 0)

    low_half = 2 * z < nz
    turns = CHUNKS + LAG
    kv_turn = (1, 4, 6)
    for i in range(turns):
        if i < CHUNKS:
            pair_sum(i)

        @pl.when(low_half)
        def _():
            if i < CHUNKS:
                chain_e(i)
            if i >= LAG:
                chain_r(i - LAG)

        @pl.when(jnp.logical_not(low_half))
        def _():
            if i < CHUNKS:
                chain_r(i)
            if i >= LAG:
                chain_e(i - LAG)

        if i in kv_turn:
            j = kv_turn.index(i)
            for k in range(j, nz - 1 if i == kv_turn[-1] else min(j + 1, nz - 1)):
                kv_step(k)
        if i == 2:
            within(cx, cb, cc, cols_c, rows_c, within_c)
        if i >= LAG:
            settle(i - LAG)
        if i >= 6:
            attend_own((i - 6) * q_heads // (turns - 6), (i - 5) * q_heads // (turns - 6))

    def finish(g, carry):
        lanes = pl.ds(pl.multiple_of(g * gw, gw), gw)
        off = pl.ds(pl.multiple_of(g * NS, NS), NS)
        for which, (x_ref, z_ref, c_ref, wi, gr, out) in enumerate(
            ((px, pz, pc, within_p, grow_p, out_p), (cx, cz, cc, within_c, grow_c, out_c))
        ):
            c_rows = c_ref[:, off]
            across = jnp.concatenate(
                [nn(c_rows, state[g * half_chunks + k, which]) for k in range(half_chunks)], axis=1
            )
            rows = wi[g] + across * gr[g] + skips[g, 0:1] * x_ref[:, lanes].astype(F32)
            gate = z_ref[:, lanes].astype(F32)
            gated = rows * (gate / (1.0 + jnp.exp(-gate)))
            power = jnp.sum(gated * gated, axis=1, keepdims=True) * (1.0 / gw)
            normed = gated * lax.rsqrt(power + NORM_EPS) * gain[:, lanes]
            if which == 1:
                normed = jnp.where(real, normed, 0.0)
            out[:, lanes] = normed.astype(BF16)
        return carry

    lax.fori_loop(0, groups, finish, 0)

    kv_side(1 - y, z, 2 * links).wait_recv()
    for j in range(nz - 1):
        kv_across(j, lambda at, k: kv_side(1 - y, at, k).wait_recv())
    attend_rest()

    kv_side(y, z, 2 * links).wait_send()
    for c in range(CHUNKS):
        s_c[c].wait_send()

    @pl.when(has_up)
    def _():
        for c in range(CHUNKS):
            e_c[c].wait_send()

    @pl.when(has_dn)
    def _():
        for c in range(CHUNKS):
            r_c[c].wait_send()

    for j in range(nz - 1):
        kv_each(j, lambda d: d.wait_send(), lambda d: d.wait_send())
        kv_across(j, lambda at, k: kv_side(y, at, k).wait_send())


def code_decay(ref, c, value):
    value = jnp.broadcast_to(value, (8, value.shape[1]))
    high = value.astype(BF16)
    ref[c, NS : NS + 16] = jnp.concatenate([high, (value - high.astype(F32)).astype(BF16)], axis=0)


def shards(n, *args):
    args = list(args)
    args[10] = args[10].reshape(1, -1)
    args[11] = args[11].reshape(1, -1)
    px, pb, pd, pk = args[0], args[2], args[4], args[16]
    steps, hp = px.shape
    groups = pb.shape[1] // NS
    heads = pd.shape[0]
    gw = hp // groups
    per = heads // groups
    cw = hp // CHUNKS
    q_heads = args[13].shape[1] // DH
    nz = n // 2
    full = pl.BlockSpec(memory_space=pltpu.VMEM)
    in_specs = [full] * len(args)
    in_specs[12] = pl.BlockSpec(memory_space=pltpu.SMEM)
    dma = pltpu.SemaphoreType.DMA
    links = max(nz - 1, 1)
    scratch = [
        pltpu.VMEM((2, nz, 2) + pk.shape, BF16),
        pltpu.VMEM((CHUNKS, NS, cw), F32),
        pltpu.VMEM((CHUNKS, NS + 16, cw), BF16),
        pltpu.VMEM((CHUNKS, NS + 16, cw), BF16),
        pltpu.VMEM((CHUNKS, NS, cw), F32),
        pltpu.VMEM((CHUNKS, NS, cw), BF16),
        pltpu.VMEM((CHUNKS, NS, cw), BF16),
        pltpu.VMEM((CHUNKS, NS + 16, cw), BF16),
        pltpu.VMEM((CHUNKS, NS + 16, cw), BF16),
        pltpu.VMEM((CHUNKS, 2, NS, cw), BF16),
        pltpu.VMEM((q_heads, steps, DH), F32),
        pltpu.VMEM((q_heads, steps, 1), F32),
        pltpu.VMEM((q_heads, steps, 1), F32),
        pltpu.VMEM((groups, steps, gw), F32),
        pltpu.VMEM((groups, steps, gw), F32),
        pltpu.VMEM((groups, steps, gw), F32),
        pltpu.VMEM((groups, steps, gw), F32),
        pltpu.VMEM((groups, steps, per), F32),
        pltpu.VMEM((groups, steps, per), F32),
        pltpu.VMEM((heads, steps), F32),
        pltpu.VMEM((heads, steps), F32),
        pltpu.VMEM((groups, 8, gw), F32),
        dma((2 * links + 1,)),
        dma((2 * links + 1,)),
        dma((links,)),
        dma((links,)),
        dma((links,)),
        dma((links,)),
    ] + [dma((CHUNKS,))] * 6
    out = jax.ShapeDtypeStruct(px.shape, BF16)
    return pl.pallas_call(
        functools.partial(kernel, n),
        out_shape=(out, out, out),
        in_specs=in_specs,
        out_specs=(full, full, full),
        scratch_shapes=scratch,
        compiler_params=pltpu.CompilerParams(
            collective_id=0, has_side_effects=True, vmem_limit_bytes=56 * 2**20
        ),
    )(*args)


def solution(mesh):
    rows = P(("groups", "ctx"), "head")
    cols = P("head", ("groups", "ctx"))
    in_specs = (
        (rows,) * 4
        + (cols,)
        + (rows,) * 4
        + (cols, P("head"), P("head"), P(("groups", "ctx")))
        + (rows,) * 5
    )
    return jax.shard_map(
        functools.partial(shards, mesh.shape["ctx"]),
        mesh=mesh,
        in_specs=in_specs,
        out_specs=(rows, rows, rows),
        check_vma=False,
    )
```

```python
import functools
import math

import jax
import jax.numpy as jnp
from jax import lax
from jax.experimental import pallas as pl
from jax.experimental.pallas import tpu as pltpu
from jax.sharding import PartitionSpec as P

NS = 128
DH = 128
NORM_EPS = 1e-05
CHUNKS = 4
LOG2E = 1.4426950408889634
MESH = pl.DeviceIdType.MESH
HI = lax.Precision.HIGHEST
F32 = jnp.float32
BF16 = jnp.bfloat16


def nt(a, b, precision=None):
    return lax.dot_general(
        a, b, (((1,), (1,)), ((), ())), preferred_element_type=F32, precision=precision
    )


def nn(a, b, precision=None):
    return jnp.dot(a, b, preferred_element_type=F32, precision=precision)


def kernel(
    n,
    px,
    pz,
    pb,
    pc,
    pd,
    cx,
    cz,
    cb,
    cc,
    cd,
    skip,
    gain,
    length_ref,
    q_ref,
    ck,
    cv,
    pk,
    pv,
    out_p,
    out_c,
    out_a,
    kv,
    s_own,
    s_send,
    s_in,
    pair,
    e_out,
    e_in,
    r_out,
    r_in,
    x_out,
    state,
    e_keep,
    within_p,
    within_c,
    grow_p,
    grow_c,
    cols_p,
    cols_c,
    rows_p,
    rows_c,
    skips,
    kvy_s,
    kvy_r,
    up_s,
    up_r,
    dn_s,
    dn_r,
    s_s,
    s_r,
    e_s,
    e_r,
    r_s,
    r_r,
    x_s,
    x_r,
):
    me = lax.axis_index("ctx")
    y = lax.rem(me, 2)
    z = lax.div(me, 2)
    nz = n // 2
    other = me + 1 - 2 * y
    has_up = z < nz - 1
    has_dn = z > 0
    steps = px.shape[0]
    groups = pb.shape[1] // NS
    per = pd.shape[0] // groups
    gw = px.shape[1] // groups
    width = gw // per
    cw = s_own.shape[2]
    tail_rows = s_send.shape[1] - NS

    barrier = pltpu.get_barrier_semaphore()
    pl.semaphore_signal(barrier, inc=1, device_id={"ctx": other}, device_id_type=MESH)

    @pl.when(has_up)
    def _():
        pl.semaphore_signal(barrier, inc=1, device_id={"ctx": me + 2}, device_id_type=MESH)

    @pl.when(has_dn)
    def _():
        pl.semaphore_signal(barrier, inc=1, device_id={"ctx": me - 2}, device_id_type=MESH)

    def remote(src, dst, ss, rs, to):
        return pltpu.make_async_remote_copy(
            src_ref=src,
            dst_ref=dst,
            send_sem=ss,
            recv_sem=rs,
            device_id={"ctx": to},
            device_id_type=MESH,
        )

    kv_y = remote(kv.at[me], kv.at[me], kvy_s, kvy_r, other)
    s_c = [
        remote(
            s_send.at[(1 - y) * CHUNKS + c], s_in.at[c], s_s.at[c], s_r.at[c], other
        )
        for c in range(CHUNKS)
    ]
    e_c = [remote(e_out.at[c], e_in.at[c], e_s.at[c], e_r.at[c], me + 2) for c in range(CHUNKS)]
    r_c = [remote(r_out.at[c], r_in.at[c], r_s.at[c], r_r.at[c], me - 2) for c in range(CHUNKS)]
    x_c = [
        remote(x_out.at[c], state.at[y * CHUNKS + c], x_s.at[c], x_r.at[c], other)
        for c in range(CHUNKS)
    ]

    def kv_up(j):
        at = kv.at[pl.ds(2 * (z - j), 2)]
        return remote(at, at, up_s.at[j], up_r.at[j], me + 2)

    def kv_dn(j):
        at = kv.at[pl.ds(2 * (z + j), 2)]
        return remote(at, at, dn_s.at[j], dn_r.at[j], me - 2)

    def kv_send(j):
        @pl.when(jnp.logical_and(has_up, z - j >= 0))
        def _():
            kv_up(j).start()

        @pl.when(jnp.logical_and(has_dn, z + j < nz))
        def _():
            kv_dn(j).start()

    def kv_recv(j):
        @pl.when(z - 1 - j >= 0)
        def _():
            at = kv.at[pl.ds(2 * (z - 1 - j), 2)]
            remote(at, at, up_s.at[j], up_r.at[j], me + 2).wait_recv()

        @pl.when(z + 1 + j < nz)
        def _():
            at = kv.at[pl.ds(2 * (z + 1 + j), 2)]
            remote(at, at, dn_s.at[j], dn_r.at[j], me - 2).wait_recv()

    kv[me, 0] = pk[...]
    kv[me, 1] = pv[...]
    t_at = lax.broadcasted_iota(jnp.int32, (steps, steps), 0)
    s_at = lax.broadcasted_iota(jnp.int32, (steps, steps), 1)
    later = t_at >= s_at
    tri = jnp.where(later, 1.0, 0.0)
    spread = jnp.where(
        lax.broadcasted_iota(jnp.int32, (per, gw), 1) // width
        == lax.broadcasted_iota(jnp.int32, (per, gw), 0),
        1.0,
        0.0,
    )
    rows_p[...] = nt(pd[...], tri, HI)
    rows_c[...] = nt(cd[...], tri, HI)
    half_chunks = gw // cw
    for g in range(groups):
        col = nt(tri, pd[g * per : (g + 1) * per, :], HI)
        cols_p[g] = col
        cols_c[g] = nt(tri, cd[g * per : (g + 1) * per, :], HI)
        grow = nn(jnp.exp(col), spread, HI)
        grow_p[g] = grow
        tail = nn(jnp.exp(col[steps - 1 : steps, :] - col), spread, HI)
        lanes = slice(g * gw, (g + 1) * gw)
        scaled = (px[:, lanes].astype(F32) * tail).astype(BF16)
        b_t = pb[:, g * NS : (g + 1) * NS].astype(F32).T.astype(BF16)
        local = nn(b_t, scaled)
        low = local.astype(BF16)
        last = jnp.broadcast_to(grow[steps - 1 : steps, :], (8, gw))
        last_hi = last.astype(BF16)
        last_lo = (last - last_hi.astype(F32)).astype(BF16)
        code = jnp.concatenate([last_hi, last_lo], axis=0)
        for k in range(half_chunks):
            at = g * half_chunks + k
            s_own[at] = local[:, k * cw : (k + 1) * cw]
            s_send[at, 0:NS] = low[:, k * cw : (k + 1) * cw]
            s_send[at, NS : NS + tail_rows] = code[:, k * cw : (k + 1) * cw]
        skips[g] = nn(jnp.broadcast_to(skip[:, g * per : (g + 1) * per], (8, per)), spread, HI)

    peers = 1 + jnp.where(has_up, 1, 0) + jnp.where(has_dn, 1, 0)
    pl.semaphore_wait(barrier, peers)

    s_c[0].start()
    kv_y.start()
    for c in range(1, CHUNKS):
        s_c[c].start()

    lane = lax.broadcasted_iota(jnp.int32, (steps, 2 * width), 1)

    def within(x_ref, b_ref, c_ref, cols, rows, result):
        def group(g, carry):
            off = pl.multiple_of(g * NS, NS)
            inner = nt(c_ref[:, pl.ds(off, NS)], b_ref[:, pl.ds(off, NS)])
            col = cols[g]
            row = rows[pl.ds(pl.multiple_of(g * per, per), per), :]
            for k in range(per // 2):
                mixed = []
                for h in (2 * k, 2 * k + 1):
                    gap = col[:, h : h + 1] - row[h : h + 1, :]
                    mixed.append(
                        (jnp.exp(jnp.where(later, gap, -jnp.inf)) * inner).astype(BF16)
                    )
                xs = x_ref[:, pl.ds(pl.multiple_of(g * gw + k * 2 * width, NS), 2 * width)]
                zero = jnp.zeros_like(xs)
                both = jnp.concatenate(
                    [jnp.where(lane < width, xs, zero), jnp.where(lane < width, zero, xs)], axis=0
                )
                result[g, :, k * 2 * width : (k + 1) * 2 * width] = nn(
                    jnp.concatenate(mixed, axis=1), both
                )
            return carry

        lax.fori_loop(0, groups, group, 0)

    within(px, pb, pc, cols_p, rows_p, within_p)
    for g in range(groups):
        grow_c[g] = nn(jnp.exp(cols_c[g]), spread, HI)
    within(cx, cb, cc, cols_c, rows_c, within_c)

    kv_y.wait_recv()
    kv_send(0)

    def decode(ref, c):
        return ref[c, NS : NS + 1].astype(F32) + ref[c, NS + 8 : NS + 9].astype(F32)

    def own_decay(c):
        at = y * CHUNKS + c
        return s_send[at, NS : NS + 1].astype(F32) + s_send[at, NS + 8 : NS + 9].astype(F32)

    def pair_decay(c):
        return own_decay(c) * decode(s_in, c)

    for c in range(CHUNKS):
        s_c[c].wait_recv()
        mine = s_own[y * CHUNKS + c]
        his = s_in[c, 0:NS].astype(F32)
        pair[c] = jnp.where(y == 0, his + decode(s_in, c) * mine, mine + own_decay(c) * his)

        @pl.when(jnp.logical_not(has_dn))
        def _():
            e_out[c] = pair[c].astype(BF16)
            e_keep[c] = jnp.zeros_like(e_keep[c])
            e_c[c].start()

        @pl.when(jnp.logical_not(has_up))
        def _():
            r_out[c, 0:NS] = pair[c].astype(BF16)
            code_decay(r_out, c, pair_decay(c))
            r_c[c].start()

    def chain_e(c):
        @pl.when(has_dn)
        def _():
            e_c[c].wait_recv()
            got = e_in[c].astype(F32)
            e_keep[c] = got

            @pl.when(has_up)
            def _():
                e_out[c] = (pair_decay(c) * got + pair[c]).astype(BF16)
                e_c[c].start()

    def chain_r(c):
        @pl.when(has_up)
        def _():
            r_c[c].wait_recv()

            @pl.when(has_dn)
            def _():
                after = decode(r_in, c)
                r_out[c, 0:NS] = (after * pair[c] + r_in[c, 0:NS].astype(F32)).astype(BF16)
                code_decay(r_out, c, after * pair_decay(c))
                r_c[c].start()

    def settle(c):
        at = y * CHUNKS + c
        entry = e_keep[c]
        through = pair_decay(c) * entry + pair[c]

        @pl.when(has_up)
        def _():
            x_out[c, 1] = (
                decode(r_in, c) * through + r_in[c, 0:NS].astype(F32)
            ).astype(BF16)

        @pl.when(jnp.logical_not(has_up))
        def _():
            x_out[c, 1] = through.astype(BF16)

        state[at, 1] = x_out[c, 1]
        first = entry.astype(BF16)

        @pl.when(y == 0)
        def _():
            state[at, 0] = first
            x_out[c, 0] = (own_decay(c) * entry + s_own[at]).astype(BF16)

        @pl.when(y != 0)
        def _():
            x_out[c, 0] = first
            state[at, 0] = (decode(s_in, c) * entry + s_in[c, 0:NS].astype(F32)).astype(BF16)

        x_c[c].start()

    low_half = 2 * z < nz

    @pl.when(low_half)
    def _():
        for c in range(CHUNKS):
            chain_e(c)

    @pl.when(jnp.logical_not(low_half))
    def _():
        for c in range(CHUNKS):
            chain_r(c)

    if nz > 1:
        kv_recv(0)
        if nz > 2:
            kv_send(1)

    @pl.when(low_half)
    def _():
        for c in range(CHUNKS):
            chain_r(c)
            settle(c)

    @pl.when(jnp.logical_not(low_half))
    def _():
        for c in range(CHUNKS):
            chain_e(c)
            settle(c)


    for j in range(1, nz - 1):
        kv_recv(j)
        if j + 1 < nz - 1:
            kv_send(j + 1)

    length = length_ref[0]
    real = lax.broadcasted_iota(jnp.int32, (steps, 1), 0) < length
    kv_heads = ck.shape[1] // DH
    ratio = q_ref.shape[1] // (DH * kv_heads)
    factor = DH ** (-0.5) * LOG2E
    span = math.gcd(n, 8)

    for g in range(kv_heads):
        cols = slice(g * DH, (g + 1) * DH)

        def head(j, carry):
            at = pl.ds(pl.multiple_of((g * ratio + j) * DH, DH), DH)
            q = q_ref[:, at]
            s = jnp.where(later, nt(q, ck[:, cols]), -jnp.inf)
            best = jnp.max(s, axis=1, keepdims=True)
            p = jnp.exp2((s - best) * factor)
            mass = jnp.sum(p, axis=1, keepdims=True)
            acc = nn(p.astype(BF16), cv[:, cols])

            def visit(b, part):
                best, mass, acc = part
                keys = kv[pl.ds(b * span, span), 0, :, cols].reshape(span * steps, DH)
                vals = kv[pl.ds(b * span, span), 1, :, cols].reshape(span * steps, DH)
                s = nt(q, keys)
                new = jnp.maximum(best, jnp.max(s, axis=1, keepdims=True))
                p = jnp.exp2((s - new) * factor)
                fade = jnp.exp2((best - new) * factor)
                mass = mass * fade + jnp.sum(p, axis=1, keepdims=True)
                return new, mass, acc * fade + nn(p.astype(BF16), vals)

            part = (best, mass, acc)
            if n == span:
                part = visit(0, part)
            else:
                part = lax.fori_loop(0, n // span, visit, part)
            best, mass, acc = part
            out_a[:, at] = jnp.where(real, acc / mass, 0.0).astype(BF16)
            return carry

        lax.fori_loop(0, ratio, head, 0)

    for c in range(CHUNKS):
        remote(
            x_out.at[c], state.at[(1 - y) * CHUNKS + c], x_s.at[c], x_r.at[c], other
        ).wait_recv()

    def finish(g, carry):
        lanes = pl.ds(pl.multiple_of(g * gw, gw), gw)
        off = pl.ds(pl.multiple_of(g * NS, NS), NS)
        for which, (x_ref, z_ref, c_ref, wi, gr, out) in enumerate(
            ((px, pz, pc, within_p, grow_p, out_p), (cx, cz, cc, within_c, grow_c, out_c))
        ):
            c_rows = c_ref[:, off]
            across = jnp.concatenate(
                [nn(c_rows, state[g * half_chunks + k, which]) for k in range(half_chunks)], axis=1
            )
            rows = wi[g] + across * gr[g] + skips[g, 0:1] * x_ref[:, lanes].astype(F32)
            gate = z_ref[:, lanes].astype(F32)
            gated = rows * (gate / (1.0 + jnp.exp(-gate)))
            power = jnp.sum(gated * gated, axis=1, keepdims=True) * (1.0 / gw)
            normed = gated * lax.rsqrt(power + NORM_EPS) * gain[:, lanes]
            if which == 1:
                normed = jnp.where(real, normed, 0.0)
            out[:, lanes] = normed.astype(BF16)
        return carry

    lax.fori_loop(0, groups, finish, 0)

    kv_y.wait_send()
    for c in range(CHUNKS):
        s_c[c].wait_send()
        x_c[c].wait_send()

    @pl.when(has_up)
    def _():
        for c in range(CHUNKS):
            e_c[c].wait_send()

    @pl.when(has_dn)
    def _():
        for c in range(CHUNKS):
            r_c[c].wait_send()

    for j in range(nz - 1):

        @pl.when(jnp.logical_and(has_up, z - j >= 0))
        def _():
            kv_up(j).wait_send()

        @pl.when(jnp.logical_and(has_dn, z + j < nz))
        def _():
            kv_dn(j).wait_send()


def code_decay(ref, c, value):
    value = jnp.broadcast_to(value, (8, value.shape[1]))
    high = value.astype(BF16)
    ref[c, NS : NS + 16] = jnp.concatenate([high, (value - high.astype(F32)).astype(BF16)], axis=0)


def shards(n, *args):
    args = list(args)
    args[10] = args[10].reshape(1, -1)
    args[11] = args[11].reshape(1, -1)
    px, pb, pd, pk = args[0], args[2], args[4], args[16]
    steps, hp = px.shape
    groups = pb.shape[1] // NS
    heads = pd.shape[0]
    gw = hp // groups
    per = heads // groups
    cw = hp // (2 * CHUNKS)
    nz = n // 2
    full = pl.BlockSpec(memory_space=pltpu.VMEM)
    in_specs = [full] * len(args)
    in_specs[12] = pl.BlockSpec(memory_space=pltpu.SMEM)
    dma = pltpu.SemaphoreType.DMA
    links = max(nz - 1, 1)
    scratch = [
        pltpu.VMEM((n, 2) + pk.shape, BF16),
        pltpu.VMEM((2 * CHUNKS, NS, cw), F32),
        pltpu.VMEM((2 * CHUNKS, NS + 16, cw), BF16),
        pltpu.VMEM((CHUNKS, NS + 16, cw), BF16),
        pltpu.VMEM((CHUNKS, NS, cw), F32),
        pltpu.VMEM((CHUNKS, NS, cw), BF16),
        pltpu.VMEM((CHUNKS, NS, cw), BF16),
        pltpu.VMEM((CHUNKS, NS + 16, cw), BF16),
        pltpu.VMEM((CHUNKS, NS + 16, cw), BF16),
        pltpu.VMEM((CHUNKS, 2, NS, cw), BF16),
        pltpu.VMEM((2 * CHUNKS, 2, NS, cw), BF16),
        pltpu.VMEM((CHUNKS, NS, cw), F32),
        pltpu.VMEM((groups, steps, gw), F32),
        pltpu.VMEM((groups, steps, gw), F32),
        pltpu.VMEM((groups, steps, gw), F32),
        pltpu.VMEM((groups, steps, gw), F32),
        pltpu.VMEM((groups, steps, per), F32),
        pltpu.VMEM((groups, steps, per), F32),
        pltpu.VMEM((heads, steps), F32),
        pltpu.VMEM((heads, steps), F32),
        pltpu.VMEM((groups, 8, gw), F32),
        dma,
        dma,
        dma((links,)),
        dma((links,)),
        dma((links,)),
        dma((links,)),
    ] + [dma((CHUNKS,))] * 8
    out = jax.ShapeDtypeStruct(px.shape, BF16)
    return pl.pallas_call(
        functools.partial(kernel, n),
        out_shape=(out, out, out),
        in_specs=in_specs,
        out_specs=(full, full, full),
        scratch_shapes=scratch,
        compiler_params=pltpu.CompilerParams(
            collective_id=0, has_side_effects=True, vmem_limit_bytes=56 * 2**20
        ),
    )(*args)


def solution(mesh):
    rows = P(("groups", "ctx"), "head")
    cols = P("head", ("groups", "ctx"))
    in_specs = (
        (rows,) * 4
        + (cols,)
        + (rows,) * 4
        + (cols, P("head"), P("head"), P(("groups", "ctx")))
        + (rows,) * 5
    )
    return jax.shard_map(
        functools.partial(shards, mesh.shape["ctx"]),
        mesh=mesh,
        in_specs=in_specs,
        out_specs=(rows, rows, rows),
        check_vma=False,
    )
```
